128 devices in a mesh: prow: 16 (over z, y), pcol: 8 (over x, core).
Axes of the slice: x: 4, y: 4, z: 4, core: 2. Of those that a mesh axis runs over, the one named last changes fastest.
Arguments:
- data: float32 [32768, 16384], P('prow', 'pcol'), may hold values from 0.05 to 5
- w_trans: float32 [32, 32768], P(None, ('prow', 'pcol')), as said below
- h_prior: float32 [32, 16384], P(None, 'pcol'), may hold values from 0.1 to 3
Outputs:
- h_next: float32 [32, 16384], P(None, 'pcol')
The draws below stay inside these ranges and needn't reach their ends.
Inputs may be any that keep to these rules, and one draw needn't show every extreme that they name: `w_trans`: every entry is positive.
All inputs are finite; a program needn't handle non-finite values.
Results may differ from the reference program's by a relative error of at most 0.0003.
Values sent between devices are 32-bit elements; how exact they have to be, the bound alone decides.
A program may use at most 64 MiB of HBM per device.

```python
import math
import jax
import jax.numpy as jnp
from jax import lax

RANK = 32
ROWS = 32768
COLS = 16384


def draw_w_trans(key, part):
    key = jax.random.fold_in(key, 11)
    first = jax.random.fold_in(key, 0)
    place = jnp.arange(ROWS, dtype=jnp.float32) / ROWS
    rising = jnp.exp(jnp.log(3.0) * place)[None, :]
    values = (jnp.abs(jax.random.normal(first, (RANK, ROWS), jnp.float32)) + 0.1) * rising
    return (values / RANK).astype(jnp.float32)


def level_of(stream_key, dims, cuts, low, top_value):
    def one(dim, shards_of):
        heights = jax.random.uniform(jax.random.fold_in(jax.random.fold_in(stream_key, 6), dim), (shards_of,), jnp.float32, low / len(cuts), top_value / len(cuts))
        return jnp.repeat(jnp.exp(heights), dims[dim] // shards_of).reshape((-1,) + (1,) * (len(dims) - dim - 1))

    loudness = one(*cuts[0])
    for cut in cuts[1:]:
        loudness = loudness * one(*cut)
    return loudness


def setup_inputs(seed: int = 0) -> dict:
    key_list = jax.random.split(jax.random.key(seed), 4)
    return {
        "data": jnp.clip(jnp.exp(math.log(5.0) - 4.6051702 * jax.random.uniform(key_list[0], (ROWS, COLS), jnp.float32) ** level_of(key_list[0], (ROWS, COLS), ((0, 16), (1, 8)), -0.2, 0.2)), 0.05, 5.0),
        "w_trans": draw_w_trans(jax.random.fold_in(key_list[3], 71), 0),
        "h_prior": jnp.clip(jnp.exp(math.log(3.0) - 3.4011974 * jax.random.uniform(key_list[2], (RANK, COLS), jnp.float32) ** level_of(key_list[2], (RANK, COLS), ((1, 8),), -0.2, 0.2)), 0.1, 3.0),
    }


def sweep(h_start, cross, gram):
    rank = h_start.shape[0]
    block = 8
    h_now = h_start
    for first in range(0, rank, block):
        mixed = jnp.dot(gram[first:first + block], h_now, precision=lax.Precision.HIGHEST)
        olds = h_now[first:first + block]
        fresh_rows = []
        for inner in range(block):
            k = first + inner
            total = mixed[inner]
            for prior in range(inner):
                total = total + gram[k, first + prior] * (fresh_rows[prior] - olds[prior])
            fresh = jnp.maximum(olds[inner] + (cross[k] - total) / gram[k, k], 0.0)
            fresh_rows.append(fresh)
        h_now = lax.dynamic_update_slice_in_dim(h_now, jnp.stack(fresh_rows, 0), first, 0)
    return h_now


def reference(data, w_trans, h_prior):
    cross = jnp.dot(w_trans, data, precision=lax.Precision.HIGHEST)
    gram = jnp.dot(w_trans, w_trans.T, precision=lax.Precision.HIGHEST)
    return sweep(h_prior, cross, gram)
```

```python
import functools

import jax
import jax.numpy as jnp
from jax import lax
from jax.experimental import pallas as pl
from jax.experimental.pallas import tpu as pltpu
from jax.sharding import PartitionSpec as P

MESH = pl.DeviceIdType.MESH
F32 = jnp.float32
BF16 = jnp.bfloat16
HIGHEST = lax.Precision.HIGHEST
EARLY = 6
TILE = 256


def pieces(x, n):
    parts = []
    for i in range(n):
        top = x.astype(BF16)
        parts.append(top)
        if i < n - 1:
            x = x - top.astype(F32)
    return parts


def stacked(w):
    return jnp.concatenate(pieces(w, 3), axis=0)


def product(ws, d):
    both = jnp.concatenate(pieces(d, 2), axis=0)
    out = jnp.dot(jnp.concatenate([ws, ws], axis=1), both, preferred_element_type=F32)
    rank = out.shape[0] // 3
    return out[:rank] + (out[rank : 2 * rank] + out[2 * rank :])


def kernel(
    n_r, n_c, w_hbm, d_hbm, h_hbm, out_ref,
    wall, dbuf, wlate, acc, outbox, inbox, gout, gin, hold, hnew, spread,
    wsem, hsem, dsem, wsend, wrecv, gsend, grecv, psend, precv, osend, orecv,
):
    r, c = lax.axis_index("prow"), lax.axis_index("pcol")
    rank, depth = w_hbm.shape
    width = out_ref.shape[1] // n_r
    n_x = n_c // 2
    x, core = c // 2, c % 2

    def source(i):
        j = i // 2
        step = ((j + 1) // 2) * (2 * (j % 2) - 1)
        return ((x + step + n_x) % n_x) * 2 + (core + i) % 2

    def rows_copy(i):
        s = source(i)
        at = pl.ds(pl.multiple_of(s * depth, depth), depth)
        return pltpu.make_async_copy(d_hbm.at[at], dbuf.at[at], dsem.at[s])

    own_w = pltpu.make_async_copy(w_hbm, wall.at[c], wsem)
    own_w.start()
    rows_copy(0).start()

    barrier = pltpu.get_barrier_semaphore()
    for i in range(1, n_c):
        pl.semaphore_signal(barrier, inc=1, device_id=(r, (c + i) % n_c), device_id_type=MESH)
    for i in range(1, n_r):
        pl.semaphore_signal(barrier, inc=1, device_id=((r + i) % n_r, c), device_id_type=MESH)

    for i in range(1, n_c):
        rows_copy(i).start()
    own_cols = pl.ds(pl.multiple_of(r * width, width), width)
    own_h = pltpu.make_async_copy(h_hbm.at[:, own_cols], hold, hsem)
    own_h.start()
    own_w.wait()
    pl.semaphore_wait(barrier, n_c + n_r - 2)

    def w_copy(i, slot):
        return pltpu.make_async_remote_copy(
            src_ref=wall.at[c], dst_ref=wall.at[slot], send_sem=wsend.at[i], recv_sem=wrecv.at[slot],
            device_id=(r, source(i)), device_id_type=MESH,
        )

    for i in range(1, n_c):
        w_copy(i, c).start()

    acc[...] = jnp.zeros_like(acc)

    def early(i, _):
        s = source(i)

        @pl.when(i > 0)
        def _():
            w_copy(i, s).wait_recv()

        rows_copy(i).wait()
        ws = stacked(wall[s])
        at = pl.ds(pl.multiple_of(s * depth, depth), depth)
        for n in range(4):
            cols = pl.ds(n * 512, 512)
            acc[:, cols] += product(ws, dbuf[at, cols])
        return 0

    lax.fori_loop(0, EARLY, early, 0)

    for j in range(n_c - EARLY):
        s = source(EARLY + j)
        w_copy(EARLY + j, s).wait_recv()
        wlate[:, j * depth : (j + 1) * depth] = stacked(wall[s])

    def gram_step(i, g):
        w = wall[i]
        return g + lax.dot_general(w, w, (((1,), (1,)), ((), ())), precision=HIGHEST, preferred_element_type=F32)

    gram = lax.fori_loop(0, n_c, gram_step, jnp.zeros((rank, rank), F32))
    gout[...] = jnp.concatenate([gram[8 * i : 8 * i + 8] for i in range(rank // 8)], axis=1)
    gin[r] = gout[...]

    def g_copy(i, slot):
        return pltpu.make_async_remote_copy(
            src_ref=gout, dst_ref=gin.at[slot], send_sem=gsend.at[i], recv_sem=grecv.at[slot],
            device_id=((r + i) % n_r, c), device_id_type=MESH,
        )

    for i in range(1, n_r):
        g_copy(i, r).start()

    for j in range(n_c - EARLY):
        rows_copy(EARLY + j).wait()

    def p_copy(owner, slot):
        return pltpu.make_async_remote_copy(
            src_ref=outbox.at[owner], dst_ref=inbox.at[slot], send_sem=psend.at[owner], recv_sem=precv.at[slot],
            device_id=(owner, c), device_id_type=MESH,
        )

    n_tiles = out_ref.shape[1] // TILE
    per = TILE // width

    def late(i, _):
        t = (r // per + 1 + i) % n_tiles
        cols = pl.ds(pl.multiple_of(t * TILE, TILE), TILE)
        total = acc[:, cols]
        for j in range(n_c - EARLY):
            at = pl.ds(pl.multiple_of(source(EARLY + j) * depth, depth), depth)
            total = total + product(wlate[:, j * depth : (j + 1) * depth], dbuf[at, cols])
        for p in range(per):
            owner = t * per + p
            outbox[owner] = total[:, p * width : (p + 1) * width]

            @pl.when(owner != r)
            def _():
                p_copy(owner, r).start()

        return 0

    lax.fori_loop(0, n_tiles, late, 0)
    inbox[r] = outbox[r]

    def g_wait(i, _):
        g_copy(i, (r + i) % n_r).wait_recv()
        return 0

    lax.fori_loop(1, n_r, g_wait, 0)
    packed = gin[0]
    for i in range(1, n_r):
        packed = packed + gin[i]

    own_h.wait()
    lanes = lax.broadcasted_iota(jnp.int32, (8, 128), 1)
    subs = lax.broadcasted_iota(jnp.int32, (8, 128), 0)
    blocks = rank // 8
    inverse = []
    for b in range(blocks):
        diagonal = jnp.sum(jnp.where(lanes == rank * b + 8 * b + subs, packed, 0.0), axis=1, keepdims=True)
        inverse.append(jnp.broadcast_to(1.0 / diagonal, (8, width)))
    above = [jnp.zeros((8, width), F32) for _ in range(blocks)]
    for k in range(rank):
        old = jnp.broadcast_to(hold[k : k + 1, :], (8, width))
        for b in range(blocks):
            column = jnp.broadcast_to(packed[:, rank * b + k : rank * b + k + 1], (8, width)) * inverse[b]
            if 8 * b < k:
                masked = column if 8 * b + 8 <= k else jnp.where(subs < k - 8 * b, column, 0.0)
                above[b] = above[b] + masked * old
            if 8 * b + 7 > k:
                masked = column if 8 * b > k else jnp.where(subs > k - 8 * b, column, 0.0)
                spread[k, 8 * b : 8 * b + 8] = masked

    def p_wait(i, _):
        s = (r + i) % n_r
        p_copy(s, s).wait_recv()
        return 0

    lax.fori_loop(1, n_r, p_wait, 0)
    cross = inbox[0]
    for i in range(1, n_r):
        cross = cross + inbox[i]
    u = [cross[8 * b : 8 * b + 8] * inverse[b] - above[b] for b in range(blocks)]
    for k in range(rank):
        b0, s0 = k // 8, k % 8
        fresh = jnp.broadcast_to(jnp.maximum(u[b0][s0 : s0 + 1], 0.0), (8, width))
        for b in range(b0, blocks):
            if 8 * b + 7 > k:
                u[b] = u[b] - spread[k, 8 * b : 8 * b + 8] * fresh
    fresh = jnp.maximum(jnp.concatenate(u, axis=0), 0.0)
    hnew[...] = fresh
    out_ref[:, own_cols] = fresh

    def o_copy(i, slot):
        cols = pl.ds(pl.multiple_of(slot * width, width), width)
        return pltpu.make_async_remote_copy(
            src_ref=hnew, dst_ref=out_ref.at[:, cols], send_sem=osend.at[i], recv_sem=orecv.at[slot],
            device_id=((r + i) % n_r, c), device_id_type=MESH,
        )

    for i in range(1, n_r):
        o_copy(i, r).start()

    def finish(i, _):
        g_copy(i, r).wait_send()
        p_copy((r + i) % n_r, r).wait_send()
        o_copy(i, r).wait_send()
        o_copy(i, (r + i) % n_r).wait_recv()
        return 0

    lax.fori_loop(1, n_r, finish, 0)
    for i in range(1, n_c):
        w_copy(i, c).wait_send()


def solution(mesh):
    n_r, n_c = mesh.shape["prow"], mesh.shape["pcol"]

    def shards(data, w_trans, h_prior):
        rank, depth = w_trans.shape
        rows, cols = data.shape
        width = cols // n_r
        dma = pltpu.SemaphoreType.DMA
        return pl.pallas_call(
            functools.partial(kernel, n_r, n_c),
            out_shape=jax.ShapeDtypeStruct((rank, cols), F32),
            in_specs=[pl.BlockSpec(memory_space=pl.ANY)] * 3,
            out_specs=pl.BlockSpec(memory_space=pltpu.VMEM),
            scratch_shapes=[
                pltpu.VMEM((n_c, rank, depth), F32),
                pltpu.VMEM((rows, cols), F32),
                pltpu.VMEM((3 * rank, (n_c - EARLY) * depth), BF16),
                pltpu.VMEM((rank, cols), F32),
                pltpu.VMEM((n_r, rank, width), F32),
                pltpu.VMEM((n_r, rank, width), F32),
                pltpu.VMEM((8, rank * rank // 8), F32),
                pltpu.VMEM((n_r, 8, rank * rank // 8), F32),
                pltpu.VMEM((rank, width), F32),
                pltpu.VMEM((rank, width), F32),
                pltpu.VMEM((rank, rank, width), F32),
                dma, dma, dma((n_c,)),
                dma((n_c,)), dma((n_c,)),
                dma((n_r,)), dma((n_r,)),
                dma((n_r,)), dma((n_r,)),
                dma((n_r,)), dma((n_r,)),
            ],
            compiler_params=pltpu.CompilerParams(
                collective_id=0, has_side_effects=True, vmem_limit_bytes=40 * 2**20
            ),
            cost_estimate=pl.CostEstimate(
                flops=2 * rank * rows * cols, bytes_accessed=4 * rows * cols, transcendentals=0
            ),
        )(*(pltpu.with_memory_space_constraint(a, pltpu.HBM) for a in (w_trans, data, h_prior)))

    placed = (P("prow", "pcol"), P(None, ("prow", "pcol")), P(None, "pcol"))
    return jax.shard_map(shards, mesh=mesh, in_specs=placed, out_specs=P(None, "pcol"), check_vma=False)
```

```python
import functools

import jax
import jax.numpy as jnp
from jax import lax
from jax.experimental import pallas as pl
from jax.experimental.pallas import tpu as pltpu
from jax.sharding import PartitionSpec as P

MESH = pl.DeviceIdType.MESH
F32 = jnp.float32
BF16 = jnp.bfloat16
EARLY = 6
TILE = 256


def pieces(x, n):
    parts = []
    for i in range(n):
        top = x.astype(BF16)
        parts.append(top)
        if i < n - 1:
            x = x - top.astype(F32)
    return parts


def stacked(w):
    return jnp.concatenate(pieces(w, 3), axis=0)


def product(ws, d):
    both = jnp.concatenate(pieces(d, 2), axis=0)
    out = jnp.dot(jnp.concatenate([ws, ws], axis=1), both, preferred_element_type=F32)
    rank = out.shape[0] // 3
    return out[:rank] + (out[rank : 2 * rank] + out[2 * rank :])


def moments(ws):
    return lax.dot_general(ws, ws, (((1,), (1,)), ((), ())), preferred_element_type=F32)


def packed_gram(m):
    rank = m.shape[0] // 3
    m = m[:rank] + (m[rank : 2 * rank] + m[2 * rank :])
    m = m[:, :rank] + (m[:, rank : 2 * rank] + m[:, 2 * rank :])
    return jnp.concatenate([m[8 * b : 8 * b + 8] for b in range(rank // 8)], axis=1)


def kernel(
    n_r, n_c, w_hbm, d_hbm, h_hbm, out_ref,
    wall, dbuf, wlate, acc, mom, outbox, inbox, hold, hnew,
    wsem, hsem, dsem, greet, wsend, wrecv, psend, precv, osend, orecv,
):
    r, c = lax.axis_index("prow"), lax.axis_index("pcol")
    rank, depth = w_hbm.shape
    width = out_ref.shape[1] // n_r
    n_x = n_c // 2
    x, core = c // 2, c % 2

    def source(i):
        j = i // 2
        step = ((j + 1) // 2) * (2 * (j % 2) - 1)
        return ((x + step + n_x) % n_x) * 2 + (core + i) % 2

    def rows_copy(i):
        s = source(i)
        at = pl.ds(pl.multiple_of(s * depth, depth), depth)
        return pltpu.make_async_copy(d_hbm.at[at], dbuf.at[at], dsem.at[s])

    own_w = pltpu.make_async_copy(w_hbm, wall.at[c], wsem)
    own_w.start()
    barrier = pltpu.get_barrier_semaphore()
    for i in range(1, n_c):
        pl.semaphore_signal(barrier, inc=1, device_id=(r, source(i)), device_id_type=MESH)
    z, y = r // LINE, r % LINE
    n_z = n_r // LINE
    for i in range(1, LINE):
        pl.semaphore_signal(barrier, inc=1, device_id=(z * LINE + (y + i) % LINE, c), device_id_type=MESH)
    for i in range(1, n_z):
        pl.semaphore_signal(barrier, inc=1, device_id=((z + i) % n_z * LINE + y, c), device_id_type=MESH)

    for i in range(n_c):
        rows_copy(i).start()
    own_cols = pl.ds(pl.multiple_of(r * width, width), width)
    own_h = pltpu.make_async_copy(h_hbm.at[:, own_cols], hold, hsem)
    own_h.start()
    own_w.wait()
    pl.semaphore_wait(barrier, n_c + LINE + n_z - 3)

    def w_copy(i, slot):
        return pltpu.make_async_remote_copy(
            src_ref=wall.at[c], dst_ref=wall.at[slot], send_sem=wsend.at[i], recv_sem=wrecv.at[slot],
            device_id=(r, source(i)), device_id_type=MESH,
        )

    for i in (1, 6, 7, 2, 4, 3, 5):
        w_copy(i, c).start()
    for i in range(1, n_z):
        pl.semaphore_signal(greet, inc=1, device_id=((z + i) % n_z * LINE + y, c), device_id_type=MESH)

    acc[...] = jnp.zeros_like(acc)
    mom[...] = jnp.zeros_like(mom)

    def early(i, _):
        s = source(i)

        @pl.when(i > 0)
        def _():
            w_copy(i, s).wait_recv()

        rows_copy(i).wait()
        ws = stacked(wall[s])
        at = pl.ds(pl.multiple_of(s * depth, depth), depth)
        for n in range(4):
            cols = pl.ds(n * 512, 512)
            acc[:, cols] += product(ws, dbuf[at, cols])
        mom[...] += moments(ws)
        return 0

    lax.fori_loop(0, EARLY, early, 0)
    pl.semaphore_wait(greet, n_z - 1)
    for j in range(EARLY, n_c):
        rows_copy(j).wait()

    for j in range(n_c - EARLY):
        s = source(EARLY + j)
        w_copy(EARLY + j, s).wait_recv()
        wlate[:, j * depth : (j + 1) * depth] = stacked(wall[s])
    gram = packed_gram(mom[...] + moments(wlate[...]))
    for i in range(n_r):
        outbox[i, rank:] = gram

    def p_copy(owner, slot):
        return pltpu.make_async_remote_copy(
            src_ref=outbox.at[owner], dst_ref=inbox.at[slot], send_sem=psend.at[owner], recv_sem=precv.at[slot],
            device_id=(owner, c), device_id_type=MESH,
        )

    n_tiles = out_ref.shape[1] // TILE
    per = TILE // width

    def late(i, _):
        t = (r // per + n_tiles // 2 + 1 + i) % n_tiles
        cols = pl.ds(pl.multiple_of(t * TILE, TILE), TILE)
        total = acc[:, cols]
        for j in range(n_c - EARLY):
            at = pl.ds(pl.multiple_of(source(EARLY + j) * depth, depth), depth)
            total = total + product(wlate[:, j * depth : (j + 1) * depth], dbuf[at, cols])
        for p in range(per):
            owner = t * per + p
            outbox[owner, :rank] = total[:, p * width : (p + 1) * width]

            @pl.when(owner != r)
            def _():
                p_copy(owner, r).start()

        return 0

    lax.fori_loop(0, n_tiles, late, 0)
    inbox[r] = outbox[r]

    own_h.wait()

    def p_wait(i, _):
        s = (r + i) % n_r
        p_copy(s, s).wait_recv()
        return 0

    lax.fori_loop(1, n_r, p_wait, 0)

    total = inbox[0]
    for i in range(1, n_r):
        total = total + inbox[i]
    packed = total[rank:]
    lanes = lax.broadcasted_iota(jnp.int32, packed.shape, 1)
    subs = lax.broadcasted_iota(jnp.int32, (8, width), 0)
    blocks = rank // 8
    inverse = []
    for b in range(blocks):
        diagonal = jnp.sum(jnp.where(lanes == rank * b + 8 * b + subs, packed, 0.0), axis=1, keepdims=True)
        inverse.append(jnp.broadcast_to(1.0 / diagonal, (8, width)))

    def column(b, k):
        return jnp.broadcast_to(packed[:, rank * b + k : rank * b + k + 1], (8, width)) * inverse[b]

    u = [total[8 * b : 8 * b + 8] * inverse[b] for b in range(blocks)]
    lower = {}
    for k in range(rank):
        b0, s0 = k // 8, k % 8
        old = jnp.broadcast_to(hold[k : k + 1, :], (8, width))
        for b in range(blocks):
            whole = column(b, k)
            if b < b0:
                u[b] = u[b] - whole * old
            elif b > b0:
                lower[k, b] = whole
            else:
                if s0:
                    u[b] = u[b] - jnp.where(subs < s0, whole, 0.0) * old
                if s0 < 7:
                    lower[k, b] = jnp.where(subs > s0, whole, 0.0)
    for k in range(rank):
        b0, s0 = k // 8, k % 8
        fresh = jnp.broadcast_to(jnp.maximum(u[b0][s0 : s0 + 1], 0.0), (8, width))
        for b in range(b0, blocks):
            if (k, b) in lower:
                u[b] = u[b] - lower[k, b] * fresh
    fresh = jnp.maximum(jnp.concatenate(u, axis=0), 0.0)
    hnew[...] = fresh

    def o_copy(i, slot):
        cols = pl.ds(pl.multiple_of(slot * width, width), width)
        return pltpu.make_async_remote_copy(
            src_ref=hnew, dst_ref=out_ref.at[:, cols], send_sem=osend.at[i], recv_sem=orecv.at[slot],
            device_id=(i, c), device_id_type=MESH,
        )

    for i in ORDER:
        @pl.when(i != r)
        def _():
            o_copy(i, r).start()

    out_ref[:, own_cols] = fresh

    def finish(i, _):
        s = (r + i) % n_r
        o_copy(s, s).wait_recv()
        p_copy(s, r).wait_send()
        o_copy(s, r).wait_send()
        return 0

    lax.fori_loop(1, n_r, finish, 0)
    for i in range(1, n_c):
        w_copy(i, c).wait_send()


LINE = 4
ORDER = (0, 1, 4, 5, 2, 3, 8, 6, 7, 9, 12, 10, 11, 13, 14, 15)


def solution(mesh):
    n_r, n_c = mesh.shape["prow"], mesh.shape["pcol"]

    def shards(data, w_trans, h_prior):
        rank, depth = w_trans.shape
        rows, cols = data.shape
        width = cols // n_r
        dma = pltpu.SemaphoreType.DMA
        return pl.pallas_call(
            functools.partial(kernel, n_r, n_c),
            out_shape=jax.ShapeDtypeStruct((rank, cols), F32),
            in_specs=[pl.BlockSpec(memory_space=pl.ANY)] * 3,
            out_specs=pl.BlockSpec(memory_space=pltpu.VMEM),
            scratch_shapes=[
                pltpu.VMEM((n_c, rank, depth), F32),
                pltpu.VMEM((rows, cols), F32),
                pltpu.VMEM((3 * rank, (n_c - EARLY) * depth), BF16),
                pltpu.VMEM((rank, cols), F32),
                pltpu.VMEM((3 * rank, 3 * rank), F32),
                pltpu.VMEM((n_r, rank + 8, width), F32),
                pltpu.VMEM((n_r, rank + 8, width), F32),
                pltpu.VMEM((rank, width), F32),
                pltpu.VMEM((rank, width), F32),
                dma, dma, dma((n_c,)), pltpu.SemaphoreType.REGULAR,
                dma((n_c,)), dma((n_c,)),
                dma((n_r,)), dma((n_r,)),
                dma((n_r,)), dma((n_r,)),
            ],
            compiler_params=pltpu.CompilerParams(
                collective_id=0, has_side_effects=True, vmem_limit_bytes=40 * 2**20
            ),
            cost_estimate=pl.CostEstimate(
                flops=2 * rank * rows * cols, bytes_accessed=4 * rows * cols, transcendentals=0
            ),
        )(*(pltpu.with_memory_space_constraint(a, pltpu.HBM) for a in (w_trans, data, h_prior)))

    placed = (P("prow", "pcol"), P(None, ("prow", "pcol")), P(None, "pcol"))
    return jax.shard_map(shards, mesh=mesh, in_specs=placed, out_specs=P(None, "pcol"), check_vma=False)
```

```python
import functools

import jax
import jax.numpy as jnp
from jax import lax
from jax.experimental import pallas as pl
from jax.experimental.pallas import tpu as pltpu
from jax.sharding import PartitionSpec as P

MESH = pl.DeviceIdType.MESH
F32 = jnp.float32
BF16 = jnp.bfloat16
EARLY = 6
TILE = 256


def pieces(x, n):
    parts = []
    for i in range(n):
        top = x.astype(BF16)
        parts.append(top)
        if i < n - 1:
            x = x - top.astype(F32)
    return parts


def stacked(w):
    return jnp.concatenate(pieces(w, 3), axis=0)


def product(ws, d):
    both = jnp.concatenate(pieces(d, 2), axis=0)
    out = jnp.dot(jnp.concatenate([ws, ws], axis=1), both, preferred_element_type=F32)
    rank = out.shape[0] // 3
    return out[:rank] + (out[rank : 2 * rank] + out[2 * rank :])


def moments(ws):
    return lax.dot_general(ws, ws, (((1,), (1,)), ((), ())), preferred_element_type=F32)


def packed_gram(m):
    rank = m.shape[0] // 3
    m = m[:rank] + (m[rank : 2 * rank] + m[2 * rank :])
    m = m[:, :rank] + (m[:, rank : 2 * rank] + m[:, 2 * rank :])
    return jnp.concatenate([m[8 * b : 8 * b + 8] for b in range(rank // 8)], axis=1)


def kernel(
    n_r, n_c, w_hbm, d_hbm, h_hbm, out_ref,
    wall, dbuf, wlate, acc, mom, outbox, inbox, hold, hnew,
    wsem, hsem, dsem, greet, wsend, wrecv, psend, precv, osend, orecv,
):
    r, c = lax.axis_index("prow"), lax.axis_index("pcol")
    rank, depth = w_hbm.shape
    width = out_ref.shape[1] // n_r
    n_x = n_c // 2
    x, core = c // 2, c % 2

    def source(i):
        j = i // 2
        step = ((j + 1) // 2) * (2 * (j % 2) - 1)
        return ((x + step + n_x) % n_x) * 2 + (core + i) % 2

    def rows_copy(j):
        chip = source(2 * j) // 2
        at = pl.ds(pl.multiple_of(chip * 2 * depth, 2 * depth), 2 * depth)
        return pltpu.make_async_copy(d_hbm.at[at], dbuf.at[at], dsem.at[j])

    own_w = pltpu.make_async_copy(w_hbm, wall.at[c], wsem)
    own_w.start()
    barrier = pltpu.get_barrier_semaphore()
    for i in range(1, n_c):
        pl.semaphore_signal(barrier, inc=1, device_id=(r, source(i)), device_id_type=MESH)
    z, y = r // LINE, r % LINE
    n_z = n_r // LINE
    for i in range(1, LINE):
        pl.semaphore_signal(barrier, inc=1, device_id=(z * LINE + (y + i) % LINE, c), device_id_type=MESH)
    for i in range(1, n_z):
        pl.semaphore_signal(barrier, inc=1, device_id=((z + i) % n_z * LINE + y, c), device_id_type=MESH)

    for j in range(n_x):
        rows_copy(j).start()
    own_cols = pl.ds(pl.multiple_of(r * width, width), width)
    own_h = pltpu.make_async_copy(h_hbm.at[:, own_cols], hold, hsem)
    own_h.start()
    own_w.wait()
    pl.semaphore_wait(barrier, n_c + LINE + n_z - 3)

    def w_copy(i, slot):
        return pltpu.make_async_remote_copy(
            src_ref=wall.at[c], dst_ref=wall.at[slot], send_sem=wsend.at[i], recv_sem=wrecv.at[slot],
            device_id=(r, source(i)), device_id_type=MESH,
        )

    for i in (1, 6, 7, 2, 4, 3, 5):
        w_copy(i, c).start()
    for i in range(1, n_z):
        pl.semaphore_signal(greet, inc=1, device_id=((z + i) % n_z * LINE + y, c), device_id_type=MESH)

    acc[...] = jnp.zeros_like(acc)
    mom[...] = jnp.zeros_like(mom)

    def early(i, _):
        s = source(i)

        @pl.when(i > 0)
        def _():
            w_copy(i, s).wait_recv()

        @pl.when(i % 2 == 0)
        def _():
            rows_copy(i // 2).wait()

        ws = stacked(wall[s])
        at = pl.ds(pl.multiple_of(s * depth, depth), depth)
        for n in range(4):
            cols = pl.ds(n * 512, 512)
            acc[:, cols] += product(ws, dbuf[at, cols])
        mom[...] += moments(ws)
        return 0

    lax.fori_loop(0, EARLY, early, 0)
    pl.semaphore_wait(greet, n_z - 1)
    for j in range(EARLY // 2, n_x):
        rows_copy(j).wait()

    for j in range(n_c - EARLY):
        s = source(EARLY + j)
        w_copy(EARLY + j, s).wait_recv()
        wlate[:, j * depth : (j + 1) * depth] = stacked(wall[s])
    gram = packed_gram(mom[...] + moments(wlate[...]))
    for i in range(n_r):
        outbox[i, rank:] = gram

    def p_copy(owner, slot):
        return pltpu.make_async_remote_copy(
            src_ref=outbox.at[owner], dst_ref=inbox.at[slot], send_sem=psend, recv_sem=precv,
            device_id=(owner, c), device_id_type=MESH,
        )

    n_tiles = out_ref.shape[1] // TILE
    per = TILE // width

    def late(i, _):
        t = (r // per + lax.shift_right_logical(FAR_FIRST, 4 * i) % 8) % n_tiles
        cols = pl.ds(pl.multiple_of(t * TILE, TILE), TILE)
        total = acc[:, cols]
        for j in range(n_c - EARLY):
            at = pl.ds(pl.multiple_of(source(EARLY + j) * depth, depth), depth)
            total = total + product(wlate[:, j * depth : (j + 1) * depth], dbuf[at, cols])
        for p in range(per):
            owner = t * per + p
            outbox[owner, :rank] = total[:, p * width : (p + 1) * width]

            @pl.when(owner != r)
            def _():
                p_copy(owner, r).start()

        return 0

    lax.fori_loop(0, n_tiles, late, 0)
    inbox[r] = outbox[r]

    own_h.wait()

    all_partials = pltpu.make_async_copy(outbox.at[1:], inbox.at[1:], precv)
    all_partials.wait()

    total = inbox[0]
    for i in range(1, n_r):
        total = total + inbox[i]
    packed = total[rank:]
    lanes = lax.broadcasted_iota(jnp.int32, packed.shape, 1)
    subs = lax.broadcasted_iota(jnp.int32, (8, width), 0)
    blocks = rank // 8
    inverse = []
    for b in range(blocks):
        diagonal = jnp.sum(jnp.where(lanes == rank * b + 8 * b + subs, packed, 0.0), axis=1, keepdims=True)
        inverse.append(jnp.broadcast_to(1.0 / diagonal, (8, width)))

    def column(b, k):
        return jnp.broadcast_to(packed[:, rank * b + k : rank * b + k + 1], (8, width)) * inverse[b]

    u = [total[8 * b : 8 * b + 8] * inverse[b] for b in range(blocks)]
    lower = {}
    for k in range(rank):
        b0, s0 = k // 8, k % 8
        old = jnp.broadcast_to(hold[k : k + 1, :], (8, width))
        for b in range(blocks):
            whole = column(b, k)
            if b < b0:
                u[b] = u[b] - whole * old
            elif b > b0:
                lower[k, b] = whole
            else:
                if s0:
                    u[b] = u[b] - jnp.where(subs < s0, whole, 0.0) * old
                if s0 < 7:
                    lower[k, b] = jnp.where(subs > s0, whole, 0.0)
    for k in range(rank):
        b0, s0 = k // 8, k % 8
        fresh = jnp.broadcast_to(jnp.maximum(u[b0][s0 : s0 + 1], 0.0), (8, width))
        for b in range(b0, blocks):
            if (k, b) in lower:
                u[b] = u[b] - lower[k, b] * fresh
    fresh = jnp.maximum(jnp.concatenate(u, axis=0), 0.0)
    hnew[...] = fresh

    def o_copy(i, slot):
        cols = pl.ds(pl.multiple_of(slot * width, width), width)
        return pltpu.make_async_remote_copy(
            src_ref=hnew, dst_ref=out_ref.at[:, cols], send_sem=osend, recv_sem=orecv,
            device_id=(i, c), device_id_type=MESH,
        )

    for i in ORDER:
        @pl.when(i != r)
        def _():
            o_copy(i, r).start()

    out_ref[:, own_cols] = fresh

    for i in range(1, n_c):
        w_copy(i, c).wait_send()
    pltpu.make_async_copy(outbox.at[1:], inbox.at[1:], psend).wait()
    others = pl.ds(0, (n_r - 1) * width)
    pltpu.make_async_copy(out_ref.at[:, others], out_ref.at[:, others], osend).wait()
    pltpu.make_async_copy(out_ref.at[:, others], out_ref.at[:, others], orecv).wait()


LINE = 4
FAR_FIRST = 0x01627345
ORDER = (0, 4, 1, 3, 2, 5, 7, 6, 8, 9, 11, 10, 12, 13, 15, 14)


def solution(mesh):
    n_r, n_c = mesh.shape["prow"], mesh.shape["pcol"]

    def shards(data, w_trans, h_prior):
        rank, depth = w_trans.shape
        rows, cols = data.shape
        width = cols // n_r
        dma = pltpu.SemaphoreType.DMA
        return pl.pallas_call(
            functools.partial(kernel, n_r, n_c),
            out_shape=jax.ShapeDtypeStruct((rank, cols), F32),
            in_specs=[pl.BlockSpec(memory_space=pl.ANY)] * 3,
            out_specs=pl.BlockSpec(memory_space=pltpu.VMEM),
            scratch_shapes=[
                pltpu.VMEM((n_c, rank, depth), F32),
                pltpu.VMEM((rows, cols), F32),
                pltpu.VMEM((3 * rank, (n_c - EARLY) * depth), BF16),
                pltpu.VMEM((rank, cols), F32),
                pltpu.VMEM((3 * rank, 3 * rank), F32),
                pltpu.VMEM((n_r, rank + 8, width), F32),
                pltpu.VMEM((n_r, rank + 8, width), F32),
                pltpu.VMEM((rank, width), F32),
                pltpu.VMEM((rank, width), F32),
                dma, dma, dma((n_c // 2,)), pltpu.SemaphoreType.REGULAR,
                dma((n_c,)), dma((n_c,)),
                dma, dma, dma, dma,
            ],
            compiler_params=pltpu.CompilerParams(
                collective_id=0, has_side_effects=True, vmem_limit_bytes=40 * 2**20
            ),
            cost_estimate=pl.CostEstimate(
                flops=2 * rank * rows * cols, bytes_accessed=4 * rows * cols, transcendentals=0
            ),
        )(*(pltpu.with_memory_space_constraint(a, pltpu.HBM) for a in (w_trans, data, h_prior)))

    placed = (P("prow", "pcol"), P(None, ("prow", "pcol")), P(None, "pcol"))
    return jax.shard_map(shards, mesh=mesh, in_specs=placed, out_specs=P(None, "pcol"), check_vma=False)
```

```python
import functools

import jax
import jax.numpy as jnp
from jax import lax
from jax.experimental import pallas as pl
from jax.experimental.pallas import tpu as pltpu
from jax.sharding import PartitionSpec as P

MESH = pl.DeviceIdType.MESH
F32 = jnp.float32
BF16 = jnp.bfloat16
EARLY = 6


def pieces(x, n):
    parts = []
    for i in range(n):
        top = x.astype(BF16)
        parts.append(top)
        if i < n - 1:
            x = x - top.astype(F32)
    return parts


def stacked(w):
    return jnp.concatenate(pieces(w, 3), axis=0)


def product(ws, d):
    both = jnp.concatenate(pieces(d, 2), axis=0)
    out = jnp.dot(jnp.concatenate([ws, ws], axis=1), both, preferred_element_type=F32)
    rank = out.shape[0] // 3
    return out[:rank] + (out[rank : 2 * rank] + out[2 * rank :])


def moments(ws):
    return lax.dot_general(ws, ws, (((1,), (1,)), ((), ())), preferred_element_type=F32)


def packed_gram(m):
    rank = m.shape[0] // 3
    m = m[:rank] + (m[rank : 2 * rank] + m[2 * rank :])
    m = m[:, :rank] + (m[:, rank : 2 * rank] + m[:, 2 * rank :])
    return jnp.concatenate([m[8 * b : 8 * b + 8] for b in range(rank // 8)], axis=1)


def kernel(
    n_r, n_c, w_hbm, d_hbm, h_hbm, out_ref,
    wall, dbuf, wlate, acc, gout, gin, grow, outbox, inbox, hold, spread, hnew,
    wsem, hsem, dsem, greet, wsend, wrecv, gsend, grecv, rsend, rrecv, psend, precv, osend, orecv,
):
    r, c = lax.axis_index("prow"), lax.axis_index("pcol")
    rank, depth = w_hbm.shape
    width = out_ref.shape[1] // n_r
    n_x = n_c // 2
    x, core = c // 2, c % 2

    def source(i):
        j = i // 2
        step = ((j + 1) // 2) * (2 * (j % 2) - 1)
        return ((x + step + n_x) % n_x) * 2 + (core + i) % 2

    def rows_copy(j):
        chip = source(2 * j) // 2
        at = pl.ds(pl.multiple_of(chip * 2 * depth, 2 * depth), 2 * depth)
        return pltpu.make_async_copy(d_hbm.at[at], dbuf.at[at], dsem.at[j])

    own_w = pltpu.make_async_copy(w_hbm, wall.at[c], wsem)
    own_w.start()
    barrier = pltpu.get_barrier_semaphore()
    for i in range(1, n_c):
        pl.semaphore_signal(barrier, inc=1, device_id=(r, source(i)), device_id_type=MESH)
    z, y = r // LINE, r % LINE
    n_z = n_r // LINE
    for i in range(1, LINE):
        pl.semaphore_signal(barrier, inc=1, device_id=(z * LINE + (y + i) % LINE, c), device_id_type=MESH)
    for i in range(1, n_z):
        pl.semaphore_signal(barrier, inc=1, device_id=((z + i) % n_z * LINE + y, c), device_id_type=MESH)

    for j in range(n_x):
        rows_copy(j).start()
    own_cols = pl.ds(pl.multiple_of(r * width, width), width)
    own_h = pltpu.make_async_copy(h_hbm.at[:, own_cols], hold, hsem)
    own_h.start()
    own_w.wait()
    pl.semaphore_wait(barrier, n_c + LINE + n_z - 3)

    def w_copy(i, slot):
        return pltpu.make_async_remote_copy(
            src_ref=wall.at[c], dst_ref=wall.at[slot], send_sem=wsend.at[i], recv_sem=wrecv.at[slot],
            device_id=(r, source(i)), device_id_type=MESH,
        )

    for i in (1, 2, 4, 3, 5, 6, 7):
        w_copy(i, c).start()
    for i in range(1, n_z):
        pl.semaphore_signal(greet, inc=1, device_id=((z + i) % n_z * LINE + y, c), device_id_type=MESH)

    acc[...] = jnp.zeros_like(acc)
    gout[...] = packed_gram(moments(stacked(wall[c])))
    gin[r] = gout[...]

    def g_copy(i):
        return pltpu.make_async_remote_copy(
            src_ref=gout, dst_ref=gin.at[r], send_sem=gsend, recv_sem=grecv,
            device_id=((r + i) % n_r, c), device_id_type=MESH,
        )

    def early(i, _):
        s = source(i)

        @pl.when(i == 2)
        def _():
            pl.semaphore_wait(greet, n_z - 1)
            for k in range(1, n_r):
                g_copy(k).start()

        @pl.when(i > 0)
        def _():
            w_copy(i, s).wait_recv()

        @pl.when(i % 2 == 0)
        def _():
            rows_copy(i // 2).wait()

        ws = stacked(wall[s])
        at = pl.ds(pl.multiple_of(s * depth, depth), depth)
        for n in range(4):
            cols = pl.ds(n * 512, 512)
            acc[:, cols] += product(ws, dbuf[at, cols])
        return 0

    lax.fori_loop(0, EARLY, early, 0)
    for j in range(EARLY // 2, n_x):
        rows_copy(j).wait()

    chip = source(EARLY) // 2
    for j in range(2):
        s = 2 * chip + j
        w_copy(EARLY, s).wait_recv()
        wlate[:, j * depth : (j + 1) * depth] = stacked(wall[s])

    def p_copy(owner, slot):
        return pltpu.make_async_remote_copy(
            src_ref=outbox.at[owner], dst_ref=inbox.at[slot], send_sem=psend, recv_sem=precv,
            device_id=(owner, c), device_id_type=MESH,
        )

    both = wlate[...]
    at = pl.ds(pl.multiple_of(source(EARLY) // 2 * 2 * depth, 2 * depth), 2 * depth)
    for dz in (2, 1, 3, 0):
        row = (z + dz) % n_z
        cols = pl.ds(pl.multiple_of(row * LINE * width, LINE * width), LINE * width)
        total = acc[:, cols] + product(both, dbuf[at, cols])
        for p in range(LINE):
            outbox[row * LINE + p] = total[:, p * width : (p + 1) * width]
        for dy in (2, 1, 3, 0):
            if dz or dy:
                p_copy(row * LINE + (y + dy) % LINE, r).start()
    inbox[r] = outbox[r]

    pltpu.make_async_copy(gin.at[1:], gin.at[1:], grecv).wait()
    packed = gin[0]
    for i in range(1, n_r):
        packed = packed + gin[i]
    grow[c] = packed

    def r_copy(i):
        return pltpu.make_async_remote_copy(
            src_ref=grow.at[c], dst_ref=grow.at[c], send_sem=rsend, recv_sem=rrecv,
            device_id=(r, source(i)), device_id_type=MESH,
        )

    for i in range(1, n_c):
        r_copy(i).start()
    own_h.wait()
    pltpu.make_async_copy(grow.at[1:], grow.at[1:], rrecv).wait()
    packed = grow[0]
    for i in range(1, n_c):
        packed = packed + grow[i]

    lanes = lax.broadcasted_iota(jnp.int32, packed.shape, 1)
    subs = lax.broadcasted_iota(jnp.int32, (8, width), 0)
    blocks = rank // 8
    inverse = []
    for b in range(blocks):
        diagonal = jnp.sum(jnp.where(lanes == rank * b + 8 * b + subs, packed, 0.0), axis=1, keepdims=True)
        inverse.append(jnp.broadcast_to(1.0 / diagonal, (8, width)))

    def column(b, k):
        return jnp.broadcast_to(packed[:, rank * b + k : rank * b + k + 1], (8, width)) * inverse[b]

    above = [jnp.zeros((8, width), F32) for _ in range(blocks)]
    lower = set()
    for k in range(rank):
        b0, s0 = k // 8, k % 8
        old = jnp.broadcast_to(hold[k : k + 1, :], (8, width))
        for b in range(blocks):
            whole = column(b, k)
            if b < b0:
                above[b] = above[b] + whole * old
            elif b == b0 and s0:
                above[b] = above[b] + jnp.where(subs < s0, whole, 0.0) * old
            if b > b0 or (b == b0 and s0 < 7):
                spread[k, 8 * b : 8 * b + 8] = whole if b > b0 else jnp.where(subs > s0, whole, 0.0)
                lower.add((k, b))

    all_partials = pltpu.make_async_copy(outbox.at[1:], inbox.at[1:], precv)
    all_partials.wait()

    total = inbox[0]
    for i in range(1, n_r):
        total = total + inbox[i]
    u = [total[8 * b : 8 * b + 8] * inverse[b] - above[b] for b in range(blocks)]
    for k in range(rank):
        b0, s0 = k // 8, k % 8
        fresh = jnp.broadcast_to(jnp.maximum(u[b0][s0 : s0 + 1], 0.0), (8, width))
        for b in range(b0, blocks):
            if (k, b) in lower:
                u[b] = u[b] - spread[k, 8 * b : 8 * b + 8] * fresh
    fresh = jnp.maximum(jnp.concatenate(u, axis=0), 0.0)
    hnew[...] = fresh

    def o_copy(i, slot):
        cols = pl.ds(pl.multiple_of(slot * width, width), width)
        return pltpu.make_async_remote_copy(
            src_ref=hnew, dst_ref=out_ref.at[:, cols], send_sem=osend, recv_sem=orecv,
            device_id=(i, c), device_id_type=MESH,
        )

    for i in ORDER:
        @pl.when(i != r)
        def _():
            o_copy(i, r).start()

    out_ref[:, own_cols] = fresh

    for i in range(1, n_c):
        w_copy(i, c).wait_send()
    pltpu.make_async_copy(gin.at[1:], gin.at[1:], gsend).wait()
    pltpu.make_async_copy(grow.at[1:], grow.at[1:], rsend).wait()
    pltpu.make_async_copy(outbox.at[1:], inbox.at[1:], psend).wait()
    others = pl.ds(0, (n_r - 1) * width)
    pltpu.make_async_copy(out_ref.at[:, others], out_ref.at[:, others], osend).wait()
    pltpu.make_async_copy(out_ref.at[:, others], out_ref.at[:, others], orecv).wait()


LINE = 4
ORDER = (0, 4, 1, 3, 2, 5, 7, 6, 8, 9, 11, 10, 12, 13, 15, 14)


def solution(mesh):
    n_r, n_c = mesh.shape["prow"], mesh.shape["pcol"]

    def shards(data, w_trans, h_prior):
        rank, depth = w_trans.shape
        rows, cols = data.shape
        width = cols // n_r
        dma = pltpu.SemaphoreType.DMA
        return pl.pallas_call(
            functools.partial(kernel, n_r, n_c),
            out_shape=jax.ShapeDtypeStruct((rank, cols), F32),
            in_specs=[pl.BlockSpec(memory_space=pl.ANY)] * 3,
            out_specs=pl.BlockSpec(memory_space=pltpu.VMEM),
            scratch_shapes=[
                pltpu.VMEM((n_c, rank, depth), F32),
                pltpu.VMEM((rows, cols), F32),
                pltpu.VMEM((3 * rank, (n_c - EARLY) * depth), BF16),
                pltpu.VMEM((rank, cols), F32),
                pltpu.VMEM((8, rank * rank // 8), F32),
                pltpu.VMEM((n_r, 8, rank * rank // 8), F32),
                pltpu.VMEM((n_c, 8, rank * rank // 8), F32),
                pltpu.VMEM((n_r, rank, width), F32),
                pltpu.VMEM((n_r, rank, width), F32),
                pltpu.VMEM((rank, width), F32),
                pltpu.VMEM((rank, rank, width), F32),
                pltpu.VMEM((rank, width), F32),
                dma, dma, dma((n_c // 2,)), pltpu.SemaphoreType.REGULAR,
                dma((n_c,)), dma((n_c,)),
                dma, dma, dma, dma,
                dma, dma, dma, dma,
            ],
            compiler_params=pltpu.CompilerParams(
                collective_id=0, has_side_effects=True, vmem_limit_bytes=40 * 2**20
            ),
            cost_estimate=pl.CostEstimate(
                flops=2 * rank * rows * cols, bytes_accessed=4 * rows * cols, transcendentals=0
            ),
        )(*(pltpu.with_memory_space_constraint(a, pltpu.HBM) for a in (w_trans, data, h_prior)))

    placed = (P("prow", "pcol"), P(None, ("prow", "pcol")), P(None, "pcol"))
    return jax.shard_map(shards, mesh=mesh, in_specs=placed, out_specs=P(None, "pcol"), check_vma=False)
```

```python
import functools

import jax
import jax.numpy as jnp
from jax import lax
from jax.experimental import pallas as pl
from jax.experimental.pallas import tpu as pltpu
from jax.sharding import PartitionSpec as P

MESH = pl.DeviceIdType.MESH
F32 = jnp.float32
BF16 = jnp.bfloat16
EARLY = 6


def pieces(x, n):
    parts = []
    for i in range(n):
        top = x.astype(BF16)
        parts.append(top)
        if i < n - 1:
            x = x - top.astype(F32)
    return parts


def stacked(w):
    return jnp.concatenate(pieces(w, 3), axis=0)


def product(ws, d):
    both = jnp.concatenate(pieces(d, 2), axis=0)
    out = jnp.dot(jnp.concatenate([ws, ws], axis=1), both, preferred_element_type=F32)
    rank = out.shape[0] // 3
    return out[:rank] + (out[rank : 2 * rank] + out[2 * rank :])


def moments(ws):
    return lax.dot_general(ws, ws, (((1,), (1,)), ((), ())), preferred_element_type=F32)


def packed_gram(m):
    rank = m.shape[0] // 3
    m = m[:rank] + (m[rank : 2 * rank] + m[2 * rank :])
    m = m[:, :rank] + (m[:, rank : 2 * rank] + m[:, 2 * rank :])
    return jnp.concatenate([m[8 * b : 8 * b + 8] for b in range(rank // 8)], axis=1)


def kernel(
    n_r, n_c, w_hbm, d_hbm, h_hbm, out_ref,
    wall, dbuf, wlate, acc, gout, gin, grow, outbox, inbox, hold, spread, hnew,
    wsem, hsem, dsem, greet, wsend, wrecv, gsend, grecv, rsend, rrecv, psend, precv, osend, orecv,
):
    r, c = lax.axis_index("prow"), lax.axis_index("pcol")
    rank, depth = w_hbm.shape
    width = out_ref.shape[1] // n_r
    n_x = n_c // 2
    x, core = c // 2, c % 2

    def source(i):
        j = i // 2
        step = ((j + 1) // 2) * (2 * (j % 2) - 1)
        return ((x + step + n_x) % n_x) * 2 + (core + i) % 2

    def rows_copy(j):
        chip = source(2 * j) // 2
        at = pl.ds(pl.multiple_of(chip * 2 * depth, 2 * depth), 2 * depth)
        return pltpu.make_async_copy(d_hbm.at[at], dbuf.at[at], dsem.at[j])

    own_w = pltpu.make_async_copy(w_hbm, wall.at[c], wsem)
    own_w.start()
    barrier = pltpu.get_barrier_semaphore()
    for i in range(1, n_c):
        pl.semaphore_signal(barrier, inc=1, device_id=(r, source(i)), device_id_type=MESH)
    z, y = r // LINE, r % LINE
    n_z = n_r // LINE
    for i in range(1, LINE):
        pl.semaphore_signal(barrier, inc=1, device_id=(z * LINE + (y + i) % LINE, c), device_id_type=MESH)
    for i in range(1, n_z):
        pl.semaphore_signal(barrier, inc=1, device_id=((z + i) % n_z * LINE + y, c), device_id_type=MESH)

    for j in range(n_x):
        rows_copy(j).start()
    own_cols = pl.ds(pl.multiple_of(r * width, width), width)
    own_h = pltpu.make_async_copy(h_hbm.at[:, own_cols], hold, hsem)
    own_h.start()
    own_w.wait()
    pl.semaphore_wait(barrier, n_c + LINE + n_z - 3)

    def w_copy(i, slot):
        return pltpu.make_async_remote_copy(
            src_ref=wall.at[c], dst_ref=wall.at[slot], send_sem=wsend.at[i], recv_sem=wrecv.at[slot],
            device_id=(r, source(i)), device_id_type=MESH,
        )

    for i in range(1, n_c):
        w_copy(i, c).start()
    for i in range(1, n_z):
        pl.semaphore_signal(greet, inc=1, device_id=((z + i) % n_z * LINE + y, c), device_id_type=MESH)

    acc[...] = jnp.zeros_like(acc)
    gout[...] = packed_gram(moments(stacked(wall[c])))
    gin[r] = gout[...]

    def g_copy(i):
        return pltpu.make_async_remote_copy(
            src_ref=gout, dst_ref=gin.at[r], send_sem=gsend, recv_sem=grecv,
            device_id=((r + i) % n_r, c), device_id_type=MESH,
        )

    def early(i, _):
        s = source(i)

        @pl.when(i == 2)
        def _():
            pl.semaphore_wait(greet, n_z - 1)
            for k in range(1, n_r):
                g_copy(k).start()

        @pl.when(i > 0)
        def _():
            w_copy(i, s).wait_recv()

        @pl.when(i % 2 == 0)
        def _():
            rows_copy(i // 2).wait()

        ws = stacked(wall[s])
        at = pl.ds(pl.multiple_of(s * depth, depth), depth)
        for n in range(4):
            cols = pl.ds(n * 512, 512)
            acc[:, cols] += product(ws, dbuf[at, cols])
        return 0

    lax.fori_loop(0, EARLY, early, 0)
    for j in range(EARLY // 2, n_x):
        rows_copy(j).wait()

    chip = source(EARLY) // 2
    for j in range(2):
        s = 2 * chip + j
        w_copy(EARLY, s).wait_recv()
        wlate[:, j * depth : (j + 1) * depth] = stacked(wall[s])

    def p_copy(owner, slot):
        return pltpu.make_async_remote_copy(
            src_ref=outbox.at[owner], dst_ref=inbox.at[slot], send_sem=psend, recv_sem=precv,
            device_id=(owner, c), device_id_type=MESH,
        )

    at = pl.ds(pl.multiple_of(source(EARLY) // 2 * 2 * depth, 2 * depth), 2 * depth)
    def late(i, _):
        row = lax.shift_right_logical(FAR_FIRST, 4 * i) % 8
        cols = pl.ds(pl.multiple_of(row * LINE * width, LINE * width), LINE * width)
        total = acc[:, cols] + product(wlate[...], dbuf[at, cols])
        for p in range(LINE):
            outbox[row * LINE + p] = total[:, p * width : (p + 1) * width]

        def send(k, _):
            piece = row * LINE + (y + lax.shift_right_logical(FAR_FIRST, 4 * k) % 8) % LINE

            @pl.when(piece != r)
            def _():
                p_copy(piece, r).start()

            return 0

        lax.fori_loop(0, LINE, send, 0)
        return 0

    lax.fori_loop(0, n_z, late, 0)
    inbox[r] = outbox[r]

    pltpu.make_async_copy(gin.at[1:], gin.at[1:], grecv).wait()
    packed = gin[0]
    for i in range(1, n_r):
        packed = packed + gin[i]
    grow[c] = packed

    def r_copy(i):
        return pltpu.make_async_remote_copy(
            src_ref=grow.at[c], dst_ref=grow.at[c], send_sem=rsend, recv_sem=rrecv,
            device_id=(r, source(i)), device_id_type=MESH,
        )

    for i in range(1, n_c):
        r_copy(i).start()
    own_h.wait()
    pltpu.make_async_copy(grow.at[1:], grow.at[1:], rrecv).wait()
    packed = grow[0]
    for i in range(1, n_c):
        packed = packed + grow[i]

    lanes = lax.broadcasted_iota(jnp.int32, packed.shape, 1)
    subs = lax.broadcasted_iota(jnp.int32, (8, width), 0)
    blocks = rank // 8
    inverse = []
    for b in range(blocks):
        diagonal = jnp.sum(jnp.where(lanes == rank * b + 8 * b + subs, packed, 0.0), axis=1, keepdims=True)
        inverse.append(jnp.broadcast_to(1.0 / diagonal, (8, width)))

    def column(b, k):
        return jnp.broadcast_to(packed[:, rank * b + k : rank * b + k + 1], (8, width)) * inverse[b]

    above = [jnp.zeros((8, width), F32) for _ in range(blocks)]
    lower = set()
    for k in range(rank):
        b0, s0 = k // 8, k % 8
        old = jnp.broadcast_to(hold[k : k + 1, :], (8, width))
        for b in range(blocks):
            whole = column(b, k)
            if b < b0:
                above[b] = above[b] + whole * old
            elif b == b0 and s0:
                above[b] = above[b] + jnp.where(subs < s0, whole, 0.0) * old
            if b > b0 or (b == b0 and s0 < 7):
                spread[k, 8 * b : 8 * b + 8] = whole if b > b0 else jnp.where(subs > s0, whole, 0.0)
                lower.add((k, b))

    all_partials = pltpu.make_async_copy(outbox.at[1:], inbox.at[1:], precv)
    all_partials.wait()

    total = inbox[0]
    for i in range(1, n_r):
        total = total + inbox[i]
    u = [total[8 * b : 8 * b + 8] * inverse[b] - above[b] for b in range(blocks)]
    for k in range(rank):
        b0, s0 = k // 8, k % 8
        fresh = jnp.broadcast_to(jnp.maximum(u[b0][s0 : s0 + 1], 0.0), (8, width))
        for b in range(b0, blocks):
            if (k, b) in lower:
                u[b] = u[b] - spread[k, 8 * b : 8 * b + 8] * fresh
    fresh = jnp.maximum(jnp.concatenate(u, axis=0), 0.0)
    hnew[...] = fresh

    def o_copy(i, slot):
        cols = pl.ds(pl.multiple_of(slot * width, width), width)
        return pltpu.make_async_remote_copy(
            src_ref=hnew, dst_ref=out_ref.at[:, cols], send_sem=osend, recv_sem=orecv,
            device_id=(i, c), device_id_type=MESH,
        )

    for i in ORDER:
        @pl.when(i != r)
        def _():
            o_copy(i, r).start()

    out_ref[:, own_cols] = fresh

    for i in range(1, n_c):
        w_copy(i, c).wait_send()
    pltpu.make_async_copy(gin.at[1:], gin.at[1:], gsend).wait()
    pltpu.make_async_copy(grow.at[1:], grow.at[1:], rsend).wait()
    pltpu.make_async_copy(outbox.at[1:], inbox.at[1:], psend).wait()
    others = pl.ds(0, (n_r - 1) * width)
    pltpu.make_async_copy(out_ref.at[:, others], out_ref.at[:, others], osend).wait()
    pltpu.make_async_copy(out_ref.at[:, others], out_ref.at[:, others], orecv).wait()


LINE = 4
FAR_FIRST = 0x0312
ORDER = (0, 4, 1, 3, 2, 5, 7, 6, 8, 9, 11, 10, 12, 13, 15, 14)


def solution(mesh):
    n_r, n_c = mesh.shape["prow"], mesh.shape["pcol"]

    def shards(data, w_trans, h_prior):
        rank, depth = w_trans.shape
        rows, cols = data.shape
        width = cols // n_r
        dma = pltpu.SemaphoreType.DMA
        return pl.pallas_call(
            functools.partial(kernel, n_r, n_c),
            out_shape=jax.ShapeDtypeStruct((rank, cols), F32),
            in_specs=[pl.BlockSpec(memory_space=pl.ANY)] * 3,
            out_specs=pl.BlockSpec(memory_space=pltpu.VMEM),
            scratch_shapes=[
                pltpu.VMEM((n_c, rank, depth), F32),
                pltpu.VMEM((rows, cols), F32),
                pltpu.VMEM((3 * rank, (n_c - EARLY) * depth), BF16),
                pltpu.VMEM((rank, cols), F32),
                pltpu.VMEM((8, rank * rank // 8), F32),
                pltpu.VMEM((n_r, 8, rank * rank // 8), F32),
                pltpu.VMEM((n_c, 8, rank * rank // 8), F32),
                pltpu.VMEM((n_r, rank, width), F32),
                pltpu.VMEM((n_r, rank, width), F32),
                pltpu.VMEM((rank, width), F32),
                pltpu.VMEM((rank, rank, width), F32),
                pltpu.VMEM((rank, width), F32),
                dma, dma, dma((n_c // 2,)), pltpu.SemaphoreType.REGULAR,
                dma((n_c,)), dma((n_c,)),
                dma, dma, dma, dma,
                dma, dma, dma, dma,
            ],
            compiler_params=pltpu.CompilerParams(
                collective_id=0, has_side_effects=True, vmem_limit_bytes=40 * 2**20
            ),
            cost_estimate=pl.CostEstimate(
                flops=2 * rank * rows * cols, bytes_accessed=4 * rows * cols, transcendentals=0
            ),
        )(*(pltpu.with_memory_space_constraint(a, pltpu.HBM) for a in (w_trans, data, h_prior)))

    placed = (P("prow", "pcol"), P(None, ("prow", "pcol")), P(None, "pcol"))
    return jax.shard_map(shards, mesh=mesh, in_specs=placed, out_specs=P(None, "pcol"), check_vma=False)
```

```python
import functools

import jax
import jax.numpy as jnp
from jax import lax
from jax.experimental import pallas as pl
from jax.experimental.pallas import tpu as pltpu
from jax.sharding import PartitionSpec as P

MESH = pl.DeviceIdType.MESH
F32 = jnp.float32
BF16 = jnp.bfloat16
EARLY = 6


def pieces(x, n):
    parts = []
    for i in range(n):
        top = x.astype(BF16)
        parts.append(top)
        if i < n - 1:
            x = x - top.astype(F32)
    return parts


def stacked(w):
    return jnp.concatenate(pieces(w, 3), axis=0)


def product(ws, d):
    both = jnp.concatenate(pieces(d, 2), axis=0)
    out = jnp.dot(jnp.concatenate([ws, ws], axis=1), both, preferred_element_type=F32)
    rank = out.shape[0] // 3
    return out[:rank] + (out[rank : 2 * rank] + out[2 * rank :])


def moments(ws):
    return lax.dot_general(ws, ws, (((1,), (1,)), ((), ())), preferred_element_type=F32)


def packed_gram(m):
    rank = m.shape[0] // 3
    m = m[:rank] + (m[rank : 2 * rank] + m[2 * rank :])
    m = m[:, :rank] + (m[:, rank : 2 * rank] + m[:, 2 * rank :])
    return jnp.concatenate([m[8 * b : 8 * b + 8] for b in range(rank // 8)], axis=1)


def kernel(
    n_r, n_c, w_hbm, d_hbm, h_hbm, out_ref,
    wall, dbuf, wlate, acc, gout, gin, grow, outbox, inbox, hold, spread, hnew,
    wsem, hsem, dsem, greet, wsend, wrecv, gsend, grecv, rsend, rrecv, psend, precv, osend, orecv,
):
    r, c = lax.axis_index("prow"), lax.axis_index("pcol")
    rank, depth = w_hbm.shape
    width = out_ref.shape[1] // n_r
    n_x = n_c // 2
    x, core = c // 2, c % 2

    def source(i):
        j = i // 2
        step = ((j + 1) // 2) * (2 * (j % 2) - 1)
        return ((x + step + n_x) % n_x) * 2 + (core + i) % 2

    def rows_copy(j):
        chip = source(2 * j) // 2
        at = pl.ds(pl.multiple_of(chip * 2 * depth, 2 * depth), 2 * depth)
        return pltpu.make_async_copy(d_hbm.at[at], dbuf.at[at], dsem.at[j])

    own_w = pltpu.make_async_copy(w_hbm, wall.at[c], wsem)
    own_w.start()
    barrier = pltpu.get_barrier_semaphore()
    for i in range(1, n_c):
        pl.semaphore_signal(barrier, inc=1, device_id=(r, source(i)), device_id_type=MESH)
    z, y = r // LINE, r % LINE
    n_z = n_r // LINE
    for i in range(1, LINE):
        pl.semaphore_signal(barrier, inc=1, device_id=(z * LINE + (y + i) % LINE, c), device_id_type=MESH)
    for i in range(1, n_z):
        pl.semaphore_signal(barrier, inc=1, device_id=((z + i) % n_z * LINE + y, c), device_id_type=MESH)

    for j in range(n_x):
        rows_copy(j).start()
    own_cols = pl.ds(pl.multiple_of(r * width, width), width)
    own_h = pltpu.make_async_copy(h_hbm.at[:, own_cols], hold, hsem)
    own_h.start()
    own_w.wait()
    pl.semaphore_wait(barrier, n_c + LINE + n_z - 3)

    def w_copy(i, slot):
        return pltpu.make_async_remote_copy(
            src_ref=wall.at[c], dst_ref=wall.at[slot], send_sem=wsend.at[i], recv_sem=wrecv.at[slot],
            device_id=(r, source(i)), device_id_type=MESH,
        )

    for i in range(1, n_c):
        w_copy(i, c).start()
    for i in range(1, n_z):
        pl.semaphore_signal(greet, inc=1, device_id=((z + i) % n_z * LINE + y, c), device_id_type=MESH)

    acc[...] = jnp.zeros_like(acc)
    gout[...] = packed_gram(moments(stacked(wall[c])))
    gin[r] = gout[...]

    def g_copy(i):
        return pltpu.make_async_remote_copy(
            src_ref=gout, dst_ref=gin.at[r], send_sem=gsend, recv_sem=grecv,
            device_id=((r + i) % n_r, c), device_id_type=MESH,
        )

    def early(i, _):
        s = source(i)

        @pl.when(i == 2)
        def _():
            pl.semaphore_wait(greet, n_z - 1)
            for k in range(1, n_r):
                g_copy(k).start()

        @pl.when(i > 0)
        def _():
            w_copy(i, s).wait_recv()

        @pl.when(i % 2 == 0)
        def _():
            rows_copy(i // 2).wait()

        ws = stacked(wall[s])
        at = pl.ds(pl.multiple_of(s * depth, depth), depth)
        for n in range(4):
            cols = pl.ds(n * 512, 512)
            acc[:, cols] += product(ws, dbuf[at, cols])
        return 0

    lax.fori_loop(0, EARLY, early, 0)
    for j in range(EARLY // 2, n_x):
        rows_copy(j).wait()

    chip = source(EARLY) // 2
    for j in range(2):
        s = 2 * chip + j
        w_copy(EARLY, s).wait_recv()
        wlate[:, j * depth : (j + 1) * depth] = stacked(wall[s])

    def p_copy(owner, slot):
        return pltpu.make_async_remote_copy(
            src_ref=outbox.at[owner], dst_ref=inbox.at[slot], send_sem=psend, recv_sem=precv,
            device_id=(owner, c), device_id_type=MESH,
        )

    at = pl.ds(pl.multiple_of(source(EARLY) // 2 * 2 * depth, 2 * depth), 2 * depth)
    def late(i, _):
        row = lax.shift_right_logical(FAR_FIRST, 4 * i) % 8
        cols = pl.ds(pl.multiple_of(row * LINE * width, LINE * width), LINE * width)
        total = acc[:, cols] + product(wlate[...], dbuf[at, cols])
        for p in range(LINE):
            outbox[row * LINE + p] = total[:, p * width : (p + 1) * width]

        def send(k, _):
            piece = row * LINE + (y + lax.shift_right_logical(FAR_FIRST, 4 * k) % 8) % LINE

            @pl.when(piece != r)
            def _():
                p_copy(piece, r).start()

            return 0

        lax.fori_loop(0, LINE, send, 0)
        return 0

    lax.fori_loop(0, n_z, late, 0)
    inbox[r] = outbox[r]

    pltpu.make_async_copy(gin.at[1:], gin.at[1:], grecv).wait()
    packed = gin[0]
    for i in range(1, n_r):
        packed = packed + gin[i]
    grow[c] = packed

    def r_copy(i):
        return pltpu.make_async_remote_copy(
            src_ref=grow.at[c], dst_ref=grow.at[c], send_sem=rsend, recv_sem=rrecv,
            device_id=(r, source(i)), device_id_type=MESH,
        )

    for i in range(1, n_c):
        r_copy(i).start()
    own_h.wait()
    pltpu.make_async_copy(grow.at[1:], grow.at[1:], rrecv).wait()
    packed = grow[0]
    for i in range(1, n_c):
        packed = packed + grow[i]

    lanes = lax.broadcasted_iota(jnp.int32, packed.shape, 1)
    subs = lax.broadcasted_iota(jnp.int32, (8, width), 0)
    blocks = rank // 8
    inverse = []
    for b in range(blocks):
        diagonal = jnp.sum(jnp.where(lanes == rank * b + 8 * b + subs, packed, 0.0), axis=1, keepdims=True)
        inverse.append(jnp.broadcast_to(1.0 / diagonal, (8, width)))

    def column(b, k):
        return jnp.broadcast_to(packed[:, rank * b + k : rank * b + k + 1], (8, width)) * inverse[b]

    above = [jnp.zeros((8, width), F32) for _ in range(blocks)]
    lower = set()
    for k in range(rank):
        b0, s0 = k // 8, k % 8
        old = jnp.broadcast_to(hold[k : k + 1, :], (8, width))
        for b in range(blocks):
            whole = column(b, k)
            if b < b0:
                above[b] = above[b] + whole * old
            elif b == b0 and s0:
                above[b] = above[b] + jnp.where(subs < s0, whole, 0.0) * old
            if b > b0 or (b == b0 and s0 < 7):
                spread[k, 8 * b : 8 * b + 8] = whole if b > b0 else jnp.where(subs > s0, whole, 0.0)
                lower.add((k, b))

    def o_copy(i, slot, first=0, n=rank):
        cols = pl.ds(pl.multiple_of(slot * width, width), width)
        return pltpu.make_async_remote_copy(
            src_ref=hnew.at[first : first + n], dst_ref=out_ref.at[first : first + n, cols], send_sem=osend, recv_sem=orecv,
            device_id=(i, c), device_id_type=MESH,
        )

    all_partials = pltpu.make_async_copy(outbox.at[1:], inbox.at[1:], precv)
    all_partials.wait()

    total = inbox[0]
    for i in range(1, n_r):
        total = total + inbox[i]
    u = [total[8 * b : 8 * b + 8] * inverse[b] - above[b] for b in range(blocks)]
    for k in range(rank):
        b0, s0 = k // 8, k % 8
        fresh = jnp.broadcast_to(jnp.maximum(u[b0][s0 : s0 + 1], 0.0), (8, width))
        for b in range(b0, blocks):
            if (k, b) in lower:
                u[b] = u[b] - spread[k, 8 * b : 8 * b + 8] * fresh
        if k == rank // 2 - 1:
            hnew[: rank // 2] = jnp.maximum(jnp.concatenate(u[: blocks // 2], axis=0), 0.0)
            for i in ORDER[:URGENT]:
                @pl.when(i != r)
                def _(i=i):
                    o_copy(i, r, 0, rank // 2).start()
    fresh = jnp.maximum(jnp.concatenate(u, axis=0), 0.0)
    hnew[rank // 2 :] = fresh[rank // 2 :]

    for i in ORDER[:URGENT]:
        @pl.when(i != r)
        def _():
            o_copy(i, r, rank // 2, rank // 2).start()

    for i in ORDER[URGENT:]:
        @pl.when(i != r)
        def _():
            o_copy(i, r).start()

    out_ref[:, own_cols] = fresh

    for i in range(1, n_c):
        w_copy(i, c).wait_send()
    pltpu.make_async_copy(gin.at[1:], gin.at[1:], gsend).wait()
    pltpu.make_async_copy(grow.at[1:], grow.at[1:], rsend).wait()
    pltpu.make_async_copy(outbox.at[1:], inbox.at[1:], psend).wait()
    others = pl.ds(0, (n_r - 1) * width)
    pltpu.make_async_copy(out_ref.at[:, others], out_ref.at[:, others], osend).wait()
    pltpu.make_async_copy(out_ref.at[:, others], out_ref.at[:, others], orecv).wait()


LINE = 4
URGENT = 1
FAR_FIRST = 0x0312
ORDER = (0, 4, 1, 3, 2, 5, 7, 6, 8, 9, 11, 10, 12, 13, 15, 14)


def solution(mesh):
    n_r, n_c = mesh.shape["prow"], mesh.shape["pcol"]

    def shards(data, w_trans, h_prior):
        rank, depth = w_trans.shape
        rows, cols = data.shape
        width = cols // n_r
        dma = pltpu.SemaphoreType.DMA
        return pl.pallas_call(
            functools.partial(kernel, n_r, n_c),
            out_shape=jax.ShapeDtypeStruct((rank, cols), F32),
            in_specs=[pl.BlockSpec(memory_space=pl.ANY)] * 3,
            out_specs=pl.BlockSpec(memory_space=pltpu.VMEM),
            scratch_shapes=[
                pltpu.VMEM((n_c, rank, depth), F32),
                pltpu.VMEM((rows, cols), F32),
                pltpu.VMEM((3 * rank, (n_c - EARLY) * depth), BF16),
                pltpu.VMEM((rank, cols), F32),
                pltpu.VMEM((8, rank * rank // 8), F32),
                pltpu.VMEM((n_r, 8, rank * rank // 8), F32),
                pltpu.VMEM((n_c, 8, rank * rank // 8), F32),
                pltpu.VMEM((n_r, rank, width), F32),
                pltpu.VMEM((n_r, rank, width), F32),
                pltpu.VMEM((rank, width), F32),
                pltpu.VMEM((rank, rank, width), F32),
                pltpu.VMEM((rank, width), F32),
                dma, dma, dma((n_c // 2,)), pltpu.SemaphoreType.REGULAR,
                dma((n_c,)), dma((n_c,)),
                dma, dma, dma, dma,
                dma, dma, dma, dma,
            ],
            compiler_params=pltpu.CompilerParams(
                collective_id=0, has_side_effects=True, vmem_limit_bytes=40 * 2**20
            ),
            cost_estimate=pl.CostEstimate(
                flops=2 * rank * rows * cols, bytes_accessed=4 * rows * cols, transcendentals=0
            ),
        )(*(pltpu.with_memory_space_constraint(a, pltpu.HBM) for a in (w_trans, data, h_prior)))

    placed = (P("prow", "pcol"), P(None, ("prow", "pcol")), P(None, "pcol"))
    return jax.shard_map(shards, mesh=mesh, in_specs=placed, out_specs=P(None, "pcol"), check_vma=False)
```
